32 devices in a mesh: sec: 8 (over y, x, core), head: 4 (over z).
Axes of the slice: x: 2, y: 2, z: 4, core: 2. Of those that a mesh axis runs over, the one named last changes fastest.
Arguments:
- tokens: bfloat16 [8192, 4096], P('sec')
- w_query: bfloat16 [4096, 4096], P(None, 'head')
- w_key: bfloat16 [4096, 1024], P(None, 'head')
- w_value: bfloat16 [4096, 1024], P(None, 'head'), may hold values from -0.09375 to 0.09375
- w_out: bfloat16 [4096, 4096], P('head'), may hold values from -0.375 to 0.375
- key_start: int32 [32], replicated, may hold values from 0 to 7936, as said below
Outputs:
- mixed: bfloat16 [8192, 4096], P('sec', 'head')
The draws below stay inside these ranges and needn't reach their ends.
Inputs may be any that keep to these rules, and one draw needn't show every extreme that they name: key_start[c] is a multiple of 256 and at most c * 256; the last block's entry is (32 - 1) * 256.
All inputs are finite; a program needn't handle non-finite values.
Results may differ from the reference program's by a relative error of at most 0.015.
The reference program's roundings to bfloat16 on the way count: a program that leaves them out, or rounds other values in their place, can miss the bound.
Values may be sent and summed in bfloat16 or wider, within the bound.
No kernel may reach another device: no remote copies, remote signals or barrier semaphores. Data moves between devices by JAX's collectives and lax.ppermute only.
A program may use at most 128 MiB of HBM per device.

```python
import math
import jax
import jax.numpy as jnp
from jax import lax

D = 4096
QH = 32
KVH = 8
HD = 128
SPAN = 256
TOKENS = 8192
NCHUNK = 32
N_HEAD = 4


def shared_query(key):
    base = jax.random.normal(jax.random.fold_in(key, 7), (D, QH * HD), jnp.float32)
    return jnp.clip(base, -6.0, 6.0) * D ** (-0.5)


def draw_tokens(key, part):
    values = jnp.clip(jax.random.normal(jax.random.fold_in(key, 1), (TOKENS, D), jnp.float32), -6.0, 6.0)
    return values.astype(jnp.bfloat16)


def draw_w_query(key, part):
    base = shared_query(key)
    return base.astype(jnp.bfloat16)


def draw_w_key(key, part):
    fresh = jax.random.normal(jax.random.fold_in(key, 9), (D, KVH * HD), jnp.float32)
    return (jnp.clip(fresh, -6.0, 6.0) * D ** (-0.5)).astype(jnp.bfloat16)


def draw_key_start(key, part):
    index = jnp.arange(NCHUNK, dtype=jnp.int32)
    drawn = jax.random.randint(jax.random.fold_in(key, 5), (NCHUNK,), 0, index + 1, dtype=jnp.int32)
    drawn = jnp.where(index == NCHUNK - 1, NCHUNK - 1, drawn)
    return drawn * SPAN


def levels(rng, dims, pieces, low, top_value):
    level, own = 1.0, jax.random.fold_in(rng, 6)
    for dim, blocks in pieces:
        heights = jnp.exp(jax.random.uniform(jax.random.fold_in(own, dim), (blocks,), jnp.float32, low / len(pieces), top_value / len(pieces)))
        level = level * jnp.repeat(heights, dims[dim] // blocks).reshape([-1 if axis == dim else 1 for axis in range(len(dims))])
    return level


def noise(own_key, extent, deviation, reach, cuts=(), kind=jnp.bfloat16):
    values = deviation * jax.random.normal(own_key, extent, jnp.float32)
    if cuts:
        values = values * levels(own_key, extent, cuts, -0.22, 0.18)
    return jnp.clip(values, -reach, reach).astype(kind)


def setup_inputs(seed: int = 0) -> dict:
    arg_keys = jax.random.split(jax.random.key(seed), 7)
    return {
        "tokens": draw_tokens(jax.random.fold_in(arg_keys[6], 71), 0),
        "w_query": draw_w_query(jax.random.fold_in(arg_keys[6], 71), 0),
        "w_key": draw_w_key(jax.random.fold_in(arg_keys[6], 71), 0),
        "w_value": noise(arg_keys[3], (D, KVH * HD), D ** -0.5, 0.09375, ((1, 4),)),
        "w_out": noise(arg_keys[4], (QH * HD, D), (2 * HD) ** -0.5, 0.375, ((0, 4),)),
        "key_start": draw_key_start(jax.random.fold_in(arg_keys[6], 71), 0),
    }


def rotate(heads_data, position):
    midway = heads_data.shape[-1] // 2
    frequency = jnp.float32(500000.0) ** (-(jnp.arange(midway, dtype=jnp.float32) * 2.0) / heads_data.shape[-1])
    angle = position.astype(jnp.float32)[:, None] * frequency[None, :]
    cosine = jnp.cos(angle)[:, None, :]
    sine = jnp.sin(angle)[:, None, :]
    first_half = heads_data[..., :midway]
    second_half = heads_data[..., midway:]
    return jnp.concatenate([first_half * cosine - second_half * sine, second_half * cosine + first_half * sine], axis=-1)


def reference(tokens, w_query, w_key, w_value, w_out, key_start):
    total = tokens.shape[0]
    groups = QH // KVH
    position = jnp.arange(total, dtype=jnp.int32)
    query = rotate(jnp.dot(tokens, w_query, preferred_element_type=jnp.float32).reshape(total, QH, HD), position).astype(jnp.bfloat16)
    keys = rotate(jnp.dot(tokens, w_key, preferred_element_type=jnp.float32).reshape(total, KVH, HD), position).astype(jnp.bfloat16)
    values = jnp.dot(tokens, w_value, preferred_element_type=jnp.float32).astype(jnp.bfloat16).reshape(total, KVH, HD)
    visible_from = jnp.repeat(key_start, SPAN)
    block = math.gcd(total, 1024)
    scale = HD ** -0.5
    outputs = []
    for index in range(total // block):
        start = index * block
        finish = start + block
        query_block = query[start:finish].reshape(block, KVH, groups, HD).transpose(1, 2, 0, 3).astype(jnp.float32)
        key_block = keys[:finish].transpose(1, 0, 2).astype(jnp.float32)
        value_block = values[:finish].transpose(1, 0, 2).astype(jnp.float32)
        query_position = position[start:finish]
        lower = visible_from[start:finish]
        key_position = position[:finish]
        allowed = (key_position[None, :] >= lower[:, None]) & (key_position[None, :] <= query_position[:, None])

        def per_group(operands):
            query_group, key_group, value_group = operands
            scores = jnp.einsum('gqd,jd->gqj', query_group, key_group) * scale
            scores = jnp.where(allowed[None], scores, -jnp.inf)
            largest = jnp.max(scores, axis=-1, keepdims=True)
            weights = jnp.exp(scores - largest)
            weight_sum = jnp.sum(weights, axis=-1, keepdims=True)
            rounded = lax.optimization_barrier(weights.astype(jnp.bfloat16)).astype(jnp.float32)
            return jnp.einsum('gqj,jd->gqd', rounded, value_group) / weight_sum

        result = lax.map(per_group, (query_block, key_block, value_block))
        outputs.append(result.transpose(2, 0, 1, 3).reshape(block, QH * HD).astype(jnp.bfloat16))
    attention = jnp.concatenate(outputs, axis=0)
    width = QH * HD // N_HEAD
    mixed = jnp.zeros((total, w_out.shape[1]), jnp.float32)
    for member in range(N_HEAD):
        term = jnp.dot(attention[:, member * width:(member + 1) * width], w_out[member * width:(member + 1) * width], preferred_element_type=jnp.float32)
        mixed = mixed + lax.optimization_barrier(term.astype(jnp.bfloat16)).astype(jnp.float32)
    return mixed.astype(jnp.bfloat16)
```

```python
import functools
import math

import jax
import jax.numpy as jnp
from jax import lax
from jax.experimental import pallas as pl
from jax.experimental.pallas import tpu as pltpu
from jax.sharding import PartitionSpec as P

QH = 32
KVH = 8
HD = 128
SPAN = 256
GROUPS = QH // KVH
WIDE = GROUPS * HD
LOG2E = math.log2(math.e)
MIB = 1 << 20


def tables(position):
    midway = HD // 2
    frequency = jnp.float32(500000.0) ** (-(jnp.arange(midway, dtype=jnp.float32) * 2.0) / HD)
    angle = position.astype(jnp.float32)[:, None] * frequency[None, :]
    cosine = jnp.cos(angle)
    sine = jnp.sin(angle)
    return jnp.concatenate([cosine, cosine], axis=1), jnp.concatenate([-sine, sine], axis=1)


def turn(block, cosine, sine):
    midway = HD // 2
    swapped = jnp.concatenate([block[:, midway:], block[:, :midway]], axis=1)
    return block * cosine + swapped * sine


def dot(a, b):
    return jnp.dot(a, b, preferred_element_type=jnp.float32)


def project_kv(tokens, w_key, w_value, cosine, sine):
    rows, depth = tokens.shape
    width = w_key.shape[1]
    count = width // HD
    tile = math.gcd(rows, 256)

    def kernel(x_ref, wk_ref, wv_ref, c_ref, s_ref, *out_refs):
        x = x_ref[...]
        keys = dot(x, wk_ref[...])
        values = dot(x, wv_ref[...])
        c, s = c_ref[...], s_ref[...]
        for h, out in enumerate(out_refs):
            part = slice(h * HD, (h + 1) * HD)
            out[:, :HD] = turn(keys[:, part], c, s).astype(jnp.bfloat16)
            out[:, HD:] = values[:, part].astype(jnp.bfloat16)

    return pl.pallas_call(
        kernel,
        grid=(rows // tile,),
        in_specs=[
            pl.BlockSpec((tile, depth), lambda i: (i, 0)),
            pl.BlockSpec((depth, width), lambda i: (0, 0)),
            pl.BlockSpec((depth, width), lambda i: (0, 0)),
            pl.BlockSpec((tile, HD), lambda i: (i, 0)),
            pl.BlockSpec((tile, HD), lambda i: (i, 0)),
        ],
        out_specs=[pl.BlockSpec((tile, 2 * HD), lambda i: (i, 0))] * count,
        out_shape=[jax.ShapeDtypeStruct((rows, 2 * HD), jnp.bfloat16)] * count,
        compiler_params=pltpu.CompilerParams(vmem_limit_bytes=40 * MIB),
        cost_estimate=pl.CostEstimate(
            flops=4 * rows * depth * width, bytes_accessed=2 * depth * (rows + 2 * width), transcendentals=0
        ),
        name="project_kv",
    )(tokens, w_key, w_value, cosine, sine)


def project_query(tokens, w_query, cosine, sine):
    rows, depth = tokens.shape
    width = w_query.shape[1]
    tile = math.gcd(rows, 256)

    def kernel(x_ref, w_ref, c_ref, s_ref, out_ref):
        x = x_ref[...]
        c, s = c_ref[...], s_ref[...]
        for h in range(0, width, 256):
            both = dot(x, w_ref[:, h : h + 256])
            for k in range(0, 256, HD):
                out_ref[:, h + k : h + k + HD] = turn(both[:, k : k + HD], c, s).astype(jnp.bfloat16)

    return pl.pallas_call(
        kernel,
        grid=(rows // tile,),
        in_specs=[
            pl.BlockSpec((tile, depth), lambda i: (i, 0)),
            pl.BlockSpec((depth, width), lambda i: (0, 0)),
            pl.BlockSpec((tile, HD), lambda i: (i, 0)),
            pl.BlockSpec((tile, HD), lambda i: (i, 0)),
        ],
        out_specs=pl.BlockSpec((tile, width), lambda i: (i, 0)),
        out_shape=jax.ShapeDtypeStruct((rows, width), jnp.bfloat16),
        compiler_params=pltpu.CompilerParams(vmem_limit_bytes=40 * MIB),
        cost_estimate=pl.CostEstimate(
            flops=2 * rows * depth * width, bytes_accessed=2 * depth * (rows + width), transcendentals=0
        ),
        name="project_query",
    )(tokens, w_query, cosine, sine)


def attend(info, query, pieces, order, group, first, number):
    rows = pieces[0].shape[0]
    count = len(pieces)
    total = rows * count
    spans = rows // SPAN
    blocks = total // SPAN
    tile = 256 if total <= 8192 else 128
    high = GROUPS * tile
    factor = HD**-0.5 * LOG2E

    def kernel(info_ref, q_ref, *refs):
        piece_refs = refs[:count]
        out_ref, kv, scores, largest, sums, gathered, sems = refs[count:]
        step = pl.program_id(0)
        own = info_ref[0]

        @pl.when(step == 0)
        def _():
            lowest = info_ref[1 + own * spans + first // SPAN]
            for extra in range(1, (number + SPAN - 1) // SPAN):
                lowest = jnp.minimum(lowest, info_ref[1 + own * spans + first // SPAN + extra])
            lowest = lowest // spans
            for k in range(count):
                at = own ^ order[k]
                copy = pltpu.make_async_copy(
                    piece_refs[k], kv.at[pl.ds(pl.multiple_of(at * rows, rows), rows)], sems.at[k]
                )

                @pl.when((at <= own) & (at >= lowest))
                def _():
                    copy.start()

            for k in range(count):
                at = own ^ order[k]
                copy = pltpu.make_async_copy(
                    piece_refs[k], kv.at[pl.ds(pl.multiple_of(at * rows, rows), rows)], sems.at[k]
                )

                @pl.when((at <= own) & (at >= lowest))
                def _():
                    copy.wait()

        offset = first + step * tile
        block = own * spans + offset // SPAN
        start = info_ref[1 + block]
        full = block - start
        q = jnp.concatenate([q_ref[:, h * HD : (h + 1) * HD] for h in range(GROUPS)], axis=0)

        def keys_at(index, size):
            return kv[pl.ds(pl.multiple_of(index * SPAN, SPAN), size), :HD]

        def values_at(index, size):
            return kv[pl.ds(pl.multiple_of(index * SPAN, SPAN), size), HD:]

        def score(keys):
            return lax.dot_general(q, keys, (((1,), (1,)), ((), ())), preferred_element_type=jnp.float32)

        own_scores = score(keys_at(block, SPAN))
        row = lax.broadcasted_iota(jnp.int32, (high, SPAN), 0) % tile + offset % SPAN
        column = lax.broadcasted_iota(jnp.int32, (high, SPAN), 1)
        own_scores = jnp.where(column <= row, own_scores, -jnp.inf)
        scores[full] = own_scores
        largest[...] = jnp.maximum(own_scores[:, :HD], own_scores[:, HD:])

        def first_pass(j, size):
            found = score(keys_at(start + j, size * SPAN))
            top = largest[...]
            for b in range(size):
                part = found[:, b * SPAN : (b + 1) * SPAN]
                scores[j + b] = part
                top = jnp.maximum(top, jnp.maximum(part[:, :HD], part[:, HD:]))
            largest[...] = top

        def pairs(number_of, body):
            def two(j, carry):
                body(2 * j, 2)
                return carry

            def one(j, carry):
                body(number_of - 1, 1)
                return carry

            lax.fori_loop(0, number_of // 2, two, 0)
            lax.fori_loop(0, number_of % 2, one, 0)

        pairs(full, first_pass)
        top = jnp.max(largest[...], axis=1, keepdims=True) * factor
        sums[...] = jnp.zeros_like(sums)
        gathered[...] = jnp.zeros_like(gathered)

        def second_pass(j, size):
            weights = []
            total_weight = sums[...]
            for b in range(size):
                part = jnp.exp2(scores[j + b] * factor - top)
                total_weight = total_weight + (part[:, :HD] + part[:, HD:])
                weights.append(part.astype(jnp.bfloat16))
            sums[...] = total_weight
            weights = jnp.concatenate(weights, axis=1)
            gathered[...] += dot(weights, values_at(start + j, size * SPAN))

        pairs(full + 1, second_pass)
        result = gathered[...] / jnp.sum(sums[...], axis=1, keepdims=True)
        result = result.astype(jnp.bfloat16)
        for h in range(GROUPS):
            out_ref[:, h * HD : (h + 1) * HD] = result[h * tile : (h + 1) * tile]

    pairs_seen = number * GROUPS * (total // 4)
    return pl.pallas_call(
        kernel,
        grid_spec=pltpu.PrefetchScalarGridSpec(
            num_scalar_prefetch=1,
            grid=(number // tile,),
            in_specs=[pl.BlockSpec((tile, WIDE), lambda i, info: (first // tile + i, group))]
            + [pl.BlockSpec(memory_space=pl.ANY)] * count,
            out_specs=pl.BlockSpec((tile, WIDE), lambda i, info: (i, 0)),
            scratch_shapes=[
                pltpu.VMEM((total, 2 * HD), jnp.bfloat16),
                pltpu.VMEM((blocks, high, SPAN), jnp.float32),
                pltpu.VMEM((high, HD), jnp.float32),
                pltpu.VMEM((high, HD), jnp.float32),
                pltpu.VMEM((high, HD), jnp.float32),
                pltpu.SemaphoreType.DMA((count,)),
            ],
        ),
        out_shape=jax.ShapeDtypeStruct((number, WIDE), jnp.bfloat16),
        compiler_params=pltpu.CompilerParams(vmem_limit_bytes=56 * MIB),
        cost_estimate=pl.CostEstimate(
            flops=4 * pairs_seen * HD * 2, bytes_accessed=total * HD * 4, transcendentals=pairs_seen
        ),
        name="attend",
    )(info, query, *pieces)


def swap(array, bit, size):
    return lax.ppermute(array, "sec", [(i, i ^ bit) for i in range(size)])


def gather_sections(own, size):
    if size == 8:
        half = own.shape[0] // 2
        across = swap(own, 2, size)
        down = swap(own, 4, size)
        far = jnp.concatenate([swap(across[:half], 4, size), swap(down[half:], 2, size)], axis=0)
        mine = [own, across, down, far]
        return mine + [swap(a, 1, size) for a in mine], [0, 2, 4, 6, 1, 3, 5, 7]
    held, order = [own], [0]
    bit = 1
    while bit < size:
        held = held + [swap(a, bit, size) for a in held]
        order = order + [k ^ bit for k in order]
        bit *= 2
    return held, order


def make_shards(sections, sets):
    def shards(tokens, w_query, w_key, w_value, w_out, key_start):
        rows = tokens.shape[0]
        local_groups = w_key.shape[1] // HD
        section = lax.axis_index("sec")
        position = section * rows + jnp.arange(rows, dtype=jnp.int32)
        cosine, sine = tables(position)
        info = jnp.concatenate([section[None].astype(jnp.int32), key_start // SPAN])
        key_values = project_kv(tokens, w_key, w_value, cosine, sine)
        gathered = [gather_sections(kv, sections) for kv in key_values]
        query = project_query(tokens, w_query, cosine, sine)
        attended = [
            attend(info, query, gathered[g][0], gathered[g][1], g, 0, rows) for g in range(local_groups)
        ]
        attended = jnp.concatenate(attended, axis=1)
        width = w_out.shape[1] // sets
        terms = [
            dot(attended, w_out[:, m * width : (m + 1) * width]).astype(jnp.bfloat16) for m in range(sets)
        ]
        terms = jnp.concatenate(terms, axis=0)
        return lax.psum_scatter(terms, "head", scatter_dimension=0, tiled=True)

    return shards


def solution(mesh):
    placed = (
        P("sec", None),
        P(None, "head"),
        P(None, "head"),
        P(None, "head"),
        P("head", None),
        P(),
    )
    return jax.shard_map(
        make_shards(mesh.shape["sec"], mesh.shape["head"]),
        mesh=mesh,
        in_specs=placed,
        out_specs=P("sec", "head"),
        check_vma=False,
    )
```

```python
import functools
import math

import jax
import jax.numpy as jnp
from jax import lax
from jax.experimental import pallas as pl
from jax.experimental.pallas import tpu as pltpu
from jax.sharding import PartitionSpec as P

QH = 32
KVH = 8
HD = 128
SPAN = 256
GROUPS = QH // KVH
WIDE = GROUPS * HD
LOG2E = math.log2(math.e)
MIB = 1 << 20
NOTES = 32
NEAR = 45.0


def work(flops):
    return pl.CostEstimate(flops=flops, bytes_accessed=0, transcendentals=0)


def tables(position):
    midway = HD // 2
    frequency = jnp.float32(500000.0) ** (-(jnp.arange(midway, dtype=jnp.float32) * 2.0) / HD)
    angle = position.astype(jnp.float32)[:, None] * frequency[None, :]
    cosine = jnp.cos(angle)
    sine = jnp.sin(angle)
    return jnp.concatenate([cosine, cosine], axis=1), jnp.concatenate([-sine, sine], axis=1)


def turn(block, cosine, sine):
    midway = HD // 2
    swapped = jnp.concatenate([block[:, midway:], block[:, :midway]], axis=1)
    return block * cosine + swapped * sine


def dot(a, b):
    return jnp.dot(a, b, preferred_element_type=jnp.float32)


def tiles(block):
    return jnp.concatenate([block[at : at + HD].T for at in range(0, block.shape[0], HD)], axis=0)


def project_kv(tokens, w_key, w_value, cosine, sine):
    rows, depth = tokens.shape
    width = w_key.shape[1]
    tile = math.gcd(rows, 256)

    def kernel(x_ref, wk_ref, wv_ref, c_ref, s_ref, out_ref, notes):
        step = pl.program_id(0)

        @pl.when(step == 0)
        def _():
            notes[...] = jnp.zeros_like(notes)

        x = x_ref[...]
        keys = dot(x, wk_ref[...])
        values = dot(x, wv_ref[...])
        c, s = c_ref[...], s_ref[...]
        here = pl.ds(pl.multiple_of(step * tile, tile), tile)
        for h in range(0, width, HD):
            key = turn(keys[:, h : h + HD], c, s)
            value = values[:, h : h + HD]
            out_ref[here, 2 * h : 2 * h + HD] = key.astype(jnp.bfloat16)
            out_ref[here, 2 * h + HD : 2 * h + 2 * HD] = tiles(value).astype(jnp.bfloat16)
            norm = jnp.max(jnp.sqrt(jnp.sum(key * key, axis=1, keepdims=True)), axis=0, keepdims=True) * 1.02
            size = jnp.max(jnp.abs(value), axis=0, keepdims=True)
            notes[:, 2 * h : 2 * h + HD] = jnp.maximum(notes[:, 2 * h : 2 * h + HD], norm)
            notes[:, 2 * h + HD : 2 * h + 2 * HD] = jnp.maximum(
                notes[:, 2 * h + HD : 2 * h + 2 * HD], size
            )

        @pl.when(step == rows // tile - 1)
        def _():
            noted = jnp.concatenate([notes[...]] * (NOTES // 8), axis=0)
            out_ref[rows:, :] = noted.astype(jnp.bfloat16)

    return pl.pallas_call(
        kernel,
        grid=(rows // tile,),
        in_specs=[
            pl.BlockSpec((tile, depth), lambda i: (i, 0)),
            pl.BlockSpec((depth, width), lambda i: (0, 0)),
            pl.BlockSpec((depth, width), lambda i: (0, 0)),
            pl.BlockSpec((tile, HD), lambda i: (i, 0)),
            pl.BlockSpec((tile, HD), lambda i: (i, 0)),
        ],
        out_specs=pl.BlockSpec((rows + NOTES, 2 * width), lambda i: (0, 0)),
        out_shape=jax.ShapeDtypeStruct((rows + NOTES, 2 * width), jnp.bfloat16),
        scratch_shapes=[pltpu.VMEM((8, 2 * width), jnp.float32)],
        compiler_params=pltpu.CompilerParams(vmem_limit_bytes=40 * MIB),
        cost_estimate=work(4 * rows * depth * width),
        name="project_kv",
    )(tokens, w_key, w_value, cosine, sine)


def project_query(tokens, w_query, cosine, sine):
    rows, depth = tokens.shape
    width = w_query.shape[1]
    tile = math.gcd(rows, 256)

    def kernel(x_ref, w_ref, c_ref, s_ref, out_ref):
        x = x_ref[...]
        c, s = c_ref[...], s_ref[...]
        for h in range(0, width, 256):
            both = dot(x, w_ref[:, h : h + 256])
            for k in range(0, 256, HD):
                turned = tiles(turn(both[:, k : k + HD], c, s))
                out_ref[:, h + k : h + k + HD] = turned.astype(jnp.bfloat16)

    return pl.pallas_call(
        kernel,
        grid=(rows // tile,),
        in_specs=[
            pl.BlockSpec((tile, depth), lambda i: (i, 0)),
            pl.BlockSpec((depth, width), lambda i: (0, 0)),
            pl.BlockSpec((tile, HD), lambda i: (i, 0)),
            pl.BlockSpec((tile, HD), lambda i: (i, 0)),
        ],
        out_specs=pl.BlockSpec((tile, width), lambda i: (i, 0)),
        out_shape=jax.ShapeDtypeStruct((rows, width), jnp.bfloat16),
        compiler_params=pltpu.CompilerParams(vmem_limit_bytes=40 * MIB),
        cost_estimate=work(2 * rows * depth * width),
        name="project_query",
    )(tokens, w_query, cosine, sine)


def tile_rows(total):
    return 256 if total <= 8192 else 128


def attend(info, query, pieces, order, first):
    rows, pair_width = pieces[0].shape
    rows = rows - NOTES
    count = len(pieces)
    total = rows * count
    spans = rows // SPAN
    blocks = total // SPAN
    local_groups = pair_width // (2 * HD)
    tile = tile_rows(total)
    high = GROUPS * tile
    factor = HD**-0.5 * LOG2E

    def kernel(info_ref, q_ref, *refs):
        piece_refs = refs[:count]
        out_ref, kv, noted, scores, sums, gathered, sems, note_sems = refs[count:]
        group = pl.program_id(0)
        own = info_ref[0]
        block = own * spans + first // SPAN
        start = info_ref[1 + block]
        lowest = start // spans

        def section_copy(k, at):
            return pltpu.make_async_copy(
                piece_refs[k].at[:rows], kv.at[pl.ds(pl.multiple_of(at * rows, rows), rows)], sems.at[at]
            )

        def note_copy(k):
            return pltpu.make_async_copy(piece_refs[k].at[rows:], noted.at[k], note_sems.at[k])

        @pl.when(group == 0)
        def _():
            for k in range(count):
                note_copy(k).start()
            for k in range(count):
                at = own ^ order[k]

                @pl.when((at <= own) & (at >= lowest))
                def _():
                    section_copy(k, at).start()

            for k in range(count):
                note_copy(k).wait()

        def arrive(at):
            @pl.when(group == 0)
            def _():
                section_copy(0, at).wait()

        key_columns = pl.ds(pl.multiple_of(group * 2 * HD, HD), HD)
        value_columns = pl.ds(pl.multiple_of(group * 2 * HD + HD, HD), HD)
        q = jnp.concatenate(
            [
                q_ref[at : at + HD, h * HD : (h + 1) * HD]
                for h in range(GROUPS)
                for at in range(0, tile, HD)
            ],
            axis=1,
        )

        def score(index, size):
            keys = kv[pl.ds(pl.multiple_of(index * SPAN, SPAN), size * SPAN), key_columns]
            return dot(keys, q) * factor

        def values_at(index, size):
            return jnp.concatenate(
                [
                    kv[pl.ds(pl.multiple_of(index * SPAN + at, HD), HD), value_columns]
                    for at in range(0, size * SPAN, HD)
                ],
                axis=1,
            )

        def own_block():
            key = lax.broadcasted_iota(jnp.int32, (SPAN, high), 0)
            row = (lax.broadcasted_iota(jnp.int32, (SPAN, high), 1) & (tile - 1)) + first % SPAN
            return jnp.where(key <= row, score(block, 1), -jnp.inf)

        def fold(array, join):
            while array.shape[0] > 8:
                middle = array.shape[0] // 2
                array = join(array[:middle], array[middle:])
            return array

        def gather(weights, index, size):
            sums[...] += fold(weights, jnp.add)
            gathered[...] += dot(values_at(index, size), weights.astype(jnp.bfloat16))

        def others(body):
            inside = jnp.maximum(start, own * spans)

            def single(j, carry):
                body(j, 1)
                return carry

            def whole(j, carry):
                at = own - 1 - j
                arrive(at)
                body(at * spans, spans)
                return carry

            lax.fori_loop(inside, block, single, 0)
            least = (start + spans - 1) // spans
            lax.fori_loop(0, own - least, whole, 0)

            @pl.when((least > lowest) & (lowest < own))
            def _():
                arrive(lowest)
                lax.fori_loop(start, least * spans, single, 0)

        q_wide = q.astype(jnp.float32)
        q_norm = jnp.max(jnp.sum(q_wide * q_wide, axis=0, keepdims=True))
        k_norm = jnp.max(noted[:, :16, key_columns].astype(jnp.float32))
        v_size = jnp.max(noted[:, :16, value_columns].astype(jnp.float32))
        bound = q_norm * (k_norm * k_norm) * (factor * factor)
        close = (bound <= NEAR * NEAR) & (v_size <= 2.0**20) & (v_size >= 2.0**-20)
        sums[...] = jnp.zeros_like(sums)
        gathered[...] = jnp.zeros_like(gathered)
        arrive(own)

        @pl.when(close)
        def _():
            found = own_block()
            base = jnp.max(found, axis=0, keepdims=True)
            gather(jnp.exp2(found - base), block, 1)
            others(lambda index, size: gather(jnp.exp2(score(index, size) - base), index, size))

        @pl.when(jnp.logical_not(close))
        def _():
            found = own_block()
            scores[block] = found
            largest = fold(found, jnp.maximum)

            def first_pass(index, size):
                for b in range(size):
                    found = score(index + b, 1)
                    scores[index + b] = found
                    sums[...] = jnp.maximum(sums[...], fold(found, jnp.maximum))

            sums[...] = largest
            others(first_pass)
            top = jnp.max(sums[...], axis=0, keepdims=True)
            sums[...] = jnp.zeros_like(sums)

            def second_pass(j, carry):
                gather(jnp.exp2(scores[j] - top), j, 1)
                return carry

            lax.fori_loop(start, block + 1, second_pass, 0)

        result = gathered[...] / jnp.sum(sums[...], axis=0, keepdims=True)
        for h in range(GROUPS):
            for at in range(0, tile, HD):
                part = result[:, h * tile + at : h * tile + at + HD]
                out_ref[at : at + HD, h * HD : (h + 1) * HD] = part.T.astype(jnp.bfloat16)

    return pl.pallas_call(
        kernel,
        grid_spec=pltpu.PrefetchScalarGridSpec(
            num_scalar_prefetch=1,
            grid=(local_groups,),
            in_specs=[pl.BlockSpec((tile, WIDE), lambda g, info: (first // tile, g))]
            + [pl.BlockSpec(memory_space=pl.ANY)] * count,
            out_specs=pl.BlockSpec((tile, WIDE), lambda g, info: (0, g)),
            scratch_shapes=[
                pltpu.VMEM((total, pair_width), jnp.bfloat16),
                pltpu.VMEM((count, NOTES, pair_width), jnp.bfloat16),
                pltpu.VMEM((blocks, SPAN, high), jnp.float32),
                pltpu.VMEM((8, high), jnp.float32),
                pltpu.VMEM((HD, high), jnp.float32),
                pltpu.SemaphoreType.DMA((count,)),
                pltpu.SemaphoreType.DMA((count,)),
            ],
        ),
        out_shape=jax.ShapeDtypeStruct((tile, local_groups * WIDE), jnp.bfloat16),
        compiler_params=pltpu.CompilerParams(vmem_limit_bytes=58 * MIB),
        cost_estimate=work(tile * local_groups * GROUPS * total * HD * 4),
        name="attend",
    )(info, query, *pieces)


def swap(array, bit, size):
    return lax.ppermute(array, "sec", [(i, i ^ bit) for i in range(size)])


def gather_sections(own, size, second=None, third=None):
    if size == 8:
        half = own.shape[0] // 2
        across = swap(own, 2, size)
        down = swap(own, 4, size)
        upper, lower = across[:half], down[half:]
        if second:
            waited = second(across, down)
            if waited:
                upper, lower = after(upper, *waited), after(lower, *waited)
        far = jnp.concatenate([swap(upper, 4, size), swap(lower, 2, size)], axis=0)
        mine = [own, across, down, far]
        if third:
            waited = third(far)
            mine = [after(a, *waited) for a in mine]
        return mine + [swap(a, 1, size) for a in mine], [0, 2, 4, 6, 1, 3, 5, 7]
    held, order = [own], [0]
    bit = 1
    while bit < size:
        held = held + [swap(a, bit, size) for a in held]
        order = order + [k ^ bit for k in order]
        bit *= 2
    return held, order


def after(array, *others):
    def kernel(*refs):
        pass

    return pl.pallas_call(
        kernel,
        in_specs=[pl.BlockSpec(memory_space=pl.ANY)] * (1 + len(others)),
        out_specs=pl.BlockSpec(memory_space=pl.ANY),
        out_shape=jax.ShapeDtypeStruct(array.shape, array.dtype),
        input_output_aliases={0: 0},
        name="after",
    )(array, *others)


def multiply(info, sources, own_weights, parcels, order, own_column, columns, partial):
    rows, depth = sources[0].shape
    width = own_weights.shape[1] // 4
    share = parcels[0].shape[0]
    count, others = len(sources), len(columns)

    def kernel(info_ref, *refs):
        source_refs, own_ref = refs[:count], refs[count]
        parcel_refs = refs[count + 1 : count + 1 + len(parcels)]
        out_ref, total, held, sems = refs[count + 1 + len(parcels) :]
        own_at = pl.multiple_of(info_ref[own_column] * width, width)
        copies = [[pltpu.make_async_copy(own_ref.at[:, pl.ds(own_at, width)], held.at[0], sems.at[0, 0])]]
        for n, column in enumerate(columns):
            copies.append([])
            for k, parcel in enumerate(parcel_refs):
                at = pl.multiple_of((info_ref[0] ^ order[k]) * share, share)
                copies[-1].append(
                    pltpu.make_async_copy(
                        parcel.at[:, column * width : (column + 1) * width],
                        held.at[n + 1, pl.ds(at, share)],
                        sems.at[n + 1, k],
                    )
                )
        for batch in copies:
            for copy in batch:
                copy.start()
        for n, batch in enumerate(copies):
            for copy in batch:
                copy.wait()
            term = dot(source_refs[n][...], held[n]).astype(jnp.bfloat16).astype(jnp.float32)
            if n == 0:
                total[...] = term
            elif n < count - 1:
                total[...] += term
            else:
                out_ref[...] = (total[...] + term).astype(out_ref.dtype)

    kind = jnp.bfloat16 if partial else jnp.float32
    return pl.pallas_call(
        kernel,
        grid_spec=pltpu.PrefetchScalarGridSpec(
            num_scalar_prefetch=1,
            grid=(1,),
            in_specs=[pl.BlockSpec((rows, depth), lambda j, info: (0, 0))] * count
            + [pl.BlockSpec(memory_space=pl.ANY)] * (1 + len(parcels)),
            out_specs=pl.BlockSpec((rows, width), lambda j, info: (0, 0)),
            scratch_shapes=[
                pltpu.VMEM((rows, width), jnp.float32),
                pltpu.VMEM((count, depth, width), jnp.bfloat16),
                pltpu.SemaphoreType.DMA((count, len(parcels))),
            ],
        ),
        out_shape=jax.ShapeDtypeStruct((rows, width), kind),
        compiler_params=pltpu.CompilerParams(vmem_limit_bytes=40 * MIB),
        cost_estimate=work(2 * rows * depth * width * count),
        name="partial" if partial else "output",
    )(info, *sources, own_weights, *parcels)


def make_shards(sections, sets):
    def shards(tokens, w_query, w_key, w_value, w_out, key_start):
        rows = tokens.shape[0]
        section = lax.axis_index("sec")
        member = lax.axis_index("head")
        position = section * rows + jnp.arange(rows, dtype=jnp.int32)
        cosine, sine = tables(position)
        info = jnp.concatenate([section[None].astype(jnp.int32), key_start // SPAN])
        own = project_kv(tokens, w_key, w_value, cosine, sine)
        query = project_query(tokens, w_query, cosine, sine)
        width = w_out.shape[1] // sets
        if sets != 4 or sections != 8:
            pieces, order = gather_sections(own, sections)
            tile = tile_rows(rows * sections)
            attended = [attend(info, query, pieces, order, at) for at in range(0, rows, tile)]
            attended = jnp.concatenate(attended, axis=0)
            terms = [
                dot(attended, w_out[:, m * width : (m + 1) * width]).astype(jnp.bfloat16)
                for m in range(sets)
            ]
            terms = jnp.concatenate(terms, axis=0)
            return lax.psum_scatter(terms, "head", scatter_dimension=0, tiled=True)

        near = [(0, 1), (3, 2)]
        middle = [(1, 2), (2, 1)]
        far = [(0, 2), (3, 1)]
        outward = [(1, 0), (2, 3)]
        left = member < 2
        share = w_out.shape[0] // sections
        mine = lax.dynamic_slice_in_dim(w_out, section * share, share, 0)
        quarter = [mine[:, m * width : (m + 1) * width] for m in range(4)]
        to_near = jnp.where(left, quarter[1], quarter[2])
        to_far = jnp.concatenate(
            [jnp.where(left, quarter[2], quarter[1]), jnp.where(left, quarter[3], quarter[0])], axis=1
        )
        parcel = [
            lax.ppermute(to_near, "head", near),
            lax.ppermute(to_far, "head", middle),
            lax.ppermute(to_far, "head", far),
        ]
        pieces, order = gather_sections(own, sections, lambda *_: (query, *parcel))
        parcel = after(jnp.concatenate(parcel, axis=1), *pieces)
        at = jnp.stack([section, member, jnp.where(left, 0, 3)]).astype(jnp.int32)

        chunk = tile_rows(rows * sections)
        held, moved = [], []

        def advance(*waited):
            i = len(held)
            if i >= 2:
                waited = waited + tuple(moved[i - 2])
            ready = after(info, *waited) if waited else info
            held.append(attend(ready, query, pieces, order, i * chunk))
            moved.append([lax.ppermute(held[i], "head", pairs) for pairs in (middle, near, far)])
            return (held[i - 1],) if i else ()

        advance()
        parcels, parcel_order = gather_sections(parcel, sections, advance, advance)
        advance(*parcels)
        results = []
        for i in range(rows // chunk):
            from_middle, from_near, from_far = moved[i]
            partial = multiply(
                at, [held[i], from_middle, from_far], w_out, parcels, parcel_order, 2, [2, 4], True
            )
            partial = lax.ppermute(partial, "head", outward)
            full = multiply(
                at,
                [held[i], from_near, from_middle, from_far],
                w_out,
                parcels,
                parcel_order,
                1,
                [0, 1, 3],
                False,
            )
            results.append((full + partial.astype(jnp.float32)).astype(jnp.bfloat16))
        return jnp.concatenate(results, axis=0)

    return shards


def solution(mesh):
    placed = (
        P("sec", None),
        P(None, "head"),
        P(None, "head"),
        P(None, "head"),
        P("head", None),
        P(),
    )
    return jax.shard_map(
        make_shards(mesh.shape["sec"], mesh.shape["head"]),
        mesh=mesh,
        in_specs=placed,
        out_specs=P("sec", "head"),
        check_vma=False,
    )
```

```python
import functools
import math

import jax
import jax.numpy as jnp
from jax import lax
from jax.experimental import pallas as pl
from jax.experimental.pallas import tpu as pltpu
from jax.sharding import PartitionSpec as P

QH = 32
KVH = 8
HD = 128
SPAN = 256
GROUPS = QH // KVH
WIDE = GROUPS * HD
LOG2E = math.log2(math.e)
MIB = 1 << 20
NOTES = 32
VMEM = 60 * MIB
NEAR = 45.0


def work(flops):
    return pl.CostEstimate(flops=flops // 8, bytes_accessed=0, transcendentals=0)


def tables(position):
    midway = HD // 2
    frequency = jnp.float32(500000.0) ** (-(jnp.arange(midway, dtype=jnp.float32) * 2.0) / HD)
    angle = position.astype(jnp.float32)[:, None] * frequency[None, :]
    cosine = jnp.cos(angle)
    sine = jnp.sin(angle)
    return jnp.concatenate([cosine, cosine], axis=1), jnp.concatenate([-sine, sine], axis=1)


def turn(block, cosine, sine):
    midway = HD // 2
    swapped = jnp.concatenate([block[:, midway:], block[:, :midway]], axis=1)
    return block * cosine + swapped * sine


def dot(a, b):
    return jnp.dot(a, b, preferred_element_type=jnp.float32)


def tiles(block):
    return jnp.concatenate([block[at : at + HD].T for at in range(0, block.shape[0], HD)], axis=0)


def project_kv(tokens, w_key, w_value, cosine, sine):
    rows, depth = tokens.shape
    width = w_key.shape[1]
    tile = math.gcd(rows, 256)

    def kernel(x_ref, wk_ref, wv_ref, c_ref, s_ref, out_ref, notes):
        step = pl.program_id(0)

        @pl.when(step == 0)
        def _():
            notes[...] = jnp.zeros_like(notes)

        x = x_ref[...]
        keys = dot(x, wk_ref[...])
        values = dot(x, wv_ref[...])
        c, s = c_ref[...], s_ref[...]
        here = pl.ds(pl.multiple_of(step * tile, tile), tile)
        for h in range(0, width, HD):
            key = turn(keys[:, h : h + HD], c, s)
            value = values[:, h : h + HD]
            out_ref[here, 2 * h : 2 * h + HD] = key.astype(jnp.bfloat16)
            out_ref[here, 2 * h + HD : 2 * h + 2 * HD] = tiles(value).astype(jnp.bfloat16)
            norm = jnp.max(jnp.sqrt(jnp.sum(key * key, axis=1, keepdims=True)), axis=0, keepdims=True) * 1.02
            size = jnp.max(jnp.abs(value), axis=0, keepdims=True)
            notes[:, 2 * h : 2 * h + HD] = jnp.maximum(notes[:, 2 * h : 2 * h + HD], norm)
            notes[:, 2 * h + HD : 2 * h + 2 * HD] = jnp.maximum(
                notes[:, 2 * h + HD : 2 * h + 2 * HD], size
            )

        @pl.when(step == rows // tile - 1)
        def _():
            noted = jnp.concatenate([notes[...]] * (NOTES // 8), axis=0)
            out_ref[rows:, :] = noted.astype(jnp.bfloat16)

    return pl.pallas_call(
        kernel,
        grid=(rows // tile,),
        in_specs=[
            pl.BlockSpec((tile, depth), lambda i: (i, 0)),
            pl.BlockSpec((depth, width), lambda i: (0, 0)),
            pl.BlockSpec((depth, width), lambda i: (0, 0)),
            pl.BlockSpec((tile, HD), lambda i: (i, 0)),
            pl.BlockSpec((tile, HD), lambda i: (i, 0)),
        ],
        out_specs=pl.BlockSpec((rows + NOTES, 2 * width), lambda i: (0, 0)),
        out_shape=jax.ShapeDtypeStruct((rows + NOTES, 2 * width), jnp.bfloat16),
        scratch_shapes=[pltpu.VMEM((8, 2 * width), jnp.float32)],
        compiler_params=pltpu.CompilerParams(vmem_limit_bytes=40 * MIB),
        cost_estimate=work(4 * rows * depth * width),
        name="project_kv",
    )(tokens, w_key, w_value, cosine, sine)


def project_query(tokens, w_query, cosine, sine):
    rows, depth = tokens.shape
    width = w_query.shape[1]
    tile = math.gcd(rows, 256)

    def kernel(x_ref, w_ref, c_ref, s_ref, out_ref):
        x = x_ref[...]
        c, s = c_ref[...], s_ref[...]
        for h in range(0, width, 256):
            both = dot(x, w_ref[:, h : h + 256])
            for k in range(0, 256, HD):
                turned = tiles(turn(both[:, k : k + HD], c, s))
                out_ref[:, h + k : h + k + HD] = turned.astype(jnp.bfloat16)

    return pl.pallas_call(
        kernel,
        grid=(rows // tile,),
        in_specs=[
            pl.BlockSpec((tile, depth), lambda i: (i, 0)),
            pl.BlockSpec((depth, width), lambda i: (0, 0)),
            pl.BlockSpec((tile, HD), lambda i: (i, 0)),
            pl.BlockSpec((tile, HD), lambda i: (i, 0)),
        ],
        out_specs=pl.BlockSpec((tile, width), lambda i: (i, 0)),
        out_shape=jax.ShapeDtypeStruct((rows, width), jnp.bfloat16),
        compiler_params=pltpu.CompilerParams(vmem_limit_bytes=VMEM),
        cost_estimate=work(2 * rows * depth * width),
        name="project_query",
    )(tokens, w_query, cosine, sine)


def tile_rows(total):
    return 256 if total <= 8192 else 128


def attend(info, query, pieces, order, first):
    rows, pair_width = pieces[0].shape
    rows = rows - NOTES
    count = len(pieces)
    total = rows * count
    spans = rows // SPAN
    blocks = total // SPAN
    local_groups = pair_width // (2 * HD)
    tile = tile_rows(total)
    high = GROUPS * tile
    factor = HD**-0.5 * LOG2E

    def kernel(info_ref, q_ref, *refs):
        piece_refs = refs[:count]
        out_ref, kv, noted, scores, sums, gathered, sems, note_sems = refs[count:]
        group = pl.program_id(0)
        own = info_ref[0]
        block = own * spans + first // SPAN
        start = info_ref[1 + block]
        lowest = start // spans

        def section_copy(k, at):
            return pltpu.make_async_copy(
                piece_refs[k].at[:rows], kv.at[pl.ds(pl.multiple_of(at * rows, rows), rows)], sems.at[at]
            )

        def note_copy(k):
            return pltpu.make_async_copy(piece_refs[k].at[rows:], noted.at[k], note_sems.at[k])

        @pl.when(group == 0)
        def _():
            for k in range(count):
                note_copy(k).start()
            for k in range(count):
                at = own ^ order[k]

                @pl.when((at <= own) & (at >= lowest))
                def _():
                    section_copy(k, at).start()

            for k in range(count):
                note_copy(k).wait()

        def arrive(at):
            @pl.when(group == 0)
            def _():
                section_copy(0, at).wait()

        key_columns = pl.ds(pl.multiple_of(group * 2 * HD, HD), HD)
        value_columns = pl.ds(pl.multiple_of(group * 2 * HD + HD, HD), HD)
        q = jnp.concatenate(
            [
                q_ref[at : at + HD, h * HD : (h + 1) * HD]
                for h in range(GROUPS)
                for at in range(0, tile, HD)
            ],
            axis=1,
        )

        def score(index, size):
            keys = kv[pl.ds(pl.multiple_of(index * SPAN, SPAN), size * SPAN), key_columns]
            return dot(keys, q) * factor

        def values_at(index, size):
            return jnp.concatenate(
                [
                    kv[pl.ds(pl.multiple_of(index * SPAN + at, HD), HD), value_columns]
                    for at in range(0, size * SPAN, HD)
                ],
                axis=1,
            )

        def own_block():
            key = lax.broadcasted_iota(jnp.int32, (SPAN, high), 0)
            row = (lax.broadcasted_iota(jnp.int32, (SPAN, high), 1) & (tile - 1)) + first % SPAN
            return jnp.where(key <= row, score(block, 1), -jnp.inf)

        def fold(array, join):
            while array.shape[0] > 8:
                middle = array.shape[0] // 2
                array = join(array[:middle], array[middle:])
            return array

        def gather(weights, index, size):
            part = sums[...]
            for at in range(0, weights.shape[0], 8):
                part = part + weights[at : at + 8]
            sums[...] = part
            gathered[...] += dot(values_at(index, size), weights.astype(jnp.bfloat16))

        def others(body):
            inside = jnp.maximum(start, own * spans)

            def single(j, carry):
                body(j, 1)
                return carry

            def whole(j, carry):
                at = own - 1 - j
                arrive(at)
                body(at * spans, spans)
                return carry

            lax.fori_loop(inside, block, single, 0)
            least = (start + spans - 1) // spans
            lax.fori_loop(0, own - least, whole, 0)

            @pl.when((least > lowest) & (lowest < own))
            def _():
                arrive(lowest)
                lax.fori_loop(start, least * spans, single, 0)

        q_wide = q.astype(jnp.float32)
        q_norm = jnp.max(jnp.sum(q_wide * q_wide, axis=0, keepdims=True))
        k_norm = jnp.max(noted[:, :16, key_columns].astype(jnp.float32))
        v_size = jnp.max(noted[:, :16, value_columns].astype(jnp.float32))
        bound = q_norm * (k_norm * k_norm) * (factor * factor)
        close = (bound <= NEAR * NEAR) & (v_size <= 2.0**20) & (v_size >= 2.0**-20)
        sums[...] = jnp.zeros_like(sums)
        gathered[...] = jnp.zeros_like(gathered)
        arrive(own)

        @pl.when(close)
        def _():
            found = own_block()
            base = jnp.max(found, axis=0, keepdims=True)
            gather(jnp.exp2(found - base), block, 1)
            others(lambda index, size: gather(jnp.exp2(score(index, size) - base), index, size))

        @pl.when(jnp.logical_not(close))
        def _():
            found = own_block()
            scores[block] = found
            largest = fold(found, jnp.maximum)

            def first_pass(index, size):
                for b in range(size):
                    found = score(index + b, 1)
                    scores[index + b] = found
                    sums[...] = jnp.maximum(sums[...], fold(found, jnp.maximum))

            sums[...] = largest
            others(first_pass)
            top = jnp.max(sums[...], axis=0, keepdims=True)
            sums[...] = jnp.zeros_like(sums)

            def second_pass(j, carry):
                gather(jnp.exp2(scores[j] - top), j, 1)
                return carry

            lax.fori_loop(start, block + 1, second_pass, 0)

        result = gathered[...] / jnp.sum(sums[...], axis=0, keepdims=True)
        for h in range(GROUPS):
            for at in range(0, tile, HD):
                part = result[:, h * tile + at : h * tile + at + HD]
                out_ref[at : at + HD, h * HD : (h + 1) * HD] = part.T.astype(jnp.bfloat16)

    return pl.pallas_call(
        kernel,
        grid_spec=pltpu.PrefetchScalarGridSpec(
            num_scalar_prefetch=1,
            grid=(local_groups,),
            in_specs=[pl.BlockSpec((tile, WIDE), lambda g, info: (first // tile, g))]
            + [pl.BlockSpec(memory_space=pl.ANY)] * count,
            out_specs=pl.BlockSpec((tile, WIDE), lambda g, info: (0, g)),
            scratch_shapes=[
                pltpu.VMEM((total, pair_width), jnp.bfloat16),
                pltpu.VMEM((count, NOTES, pair_width), jnp.bfloat16),
                pltpu.VMEM((blocks, SPAN, high), jnp.float32),
                pltpu.VMEM((8, high), jnp.float32),
                pltpu.VMEM((HD, high), jnp.float32),
                pltpu.SemaphoreType.DMA((count,)),
                pltpu.SemaphoreType.DMA((count,)),
            ],
        ),
        out_shape=jax.ShapeDtypeStruct((tile, local_groups * WIDE), jnp.bfloat16),
        compiler_params=pltpu.CompilerParams(vmem_limit_bytes=VMEM),
        cost_estimate=work(tile * local_groups * GROUPS * total * HD * 4),
        name="attend",
    )(info, query, *pieces)


def swap(array, bit, size):
    return lax.ppermute(array, "sec", [(i, i ^ bit) for i in range(size)])


def gather_sections(own, size, second=None, third=None):
    if size == 8:
        half = own.shape[0] // 2
        across = swap(own, 2, size)
        down = swap(own, 4, size)
        upper, lower = across[:half], down[half:]
        if second:
            waited = second(across, down)
            if waited:
                upper, lower = after(upper, *waited), after(lower, *waited)
        far = jnp.concatenate([swap(upper, 4, size), swap(lower, 2, size)], axis=0)
        mine = [own, across, down, far]
        if third:
            waited = third(far)
            mine = [after(a, *waited) for a in mine]
        return mine + [swap(a, 1, size) for a in mine], [0, 2, 4, 6, 1, 3, 5, 7]
    held, order = [own], [0]
    bit = 1
    while bit < size:
        held = held + [swap(a, bit, size) for a in held]
        order = order + [k ^ bit for k in order]
        bit *= 2
    return held, order


def after(array, *others):
    def kernel(*refs):
        pass

    return pl.pallas_call(
        kernel,
        in_specs=[pl.BlockSpec(memory_space=pl.ANY)] * (1 + len(others)),
        out_specs=pl.BlockSpec(memory_space=pl.ANY),
        out_shape=jax.ShapeDtypeStruct(array.shape, array.dtype),
        input_output_aliases={0: 0},
        name="after",
    )(array, *others)


def multiply(info, sources, own_weights, weights, own_column, partial):
    chunks = len(sources[0])
    depth, width = own_weights.shape[0], own_weights.shape[1] // 4
    chunk = sources[0][0][0].shape[0]
    count = len(sources)
    flat = [entry for source in sources for entry in source]

    def kernel(info_ref, *refs):
        source_refs = refs[: len(flat)]
        own_ref, weight_ref, out_ref, total, held, sems = refs[len(flat) :]
        own_at = pl.multiple_of(info_ref[own_column] * width, width)
        copies = [pltpu.make_async_copy(own_ref.at[:, pl.ds(own_at, width)], held.at[0], sems.at[0])]
        for n in range(1, count):
            block = weight_ref.at[:, (n - 1) * width : n * width]
            copies.append(pltpu.make_async_copy(block, held.at[n], sems.at[n]))
        for copy in copies:
            copy.start()
        for n, copy in enumerate(copies):
            copy.wait()
            for c in range(chunks):
                part = slice(c * chunk, (c + 1) * chunk)
                term = dot(source_refs[n * chunks + c][...], held[n])
                term = term.astype(jnp.bfloat16).astype(jnp.float32)
                if n == 0:
                    total[part] = term
                elif n < count - 1:
                    total[part] += term
                else:
                    out_ref[part] = (total[part] + term).astype(out_ref.dtype)

    rows = chunk * chunks
    kind = jnp.bfloat16 if partial else jnp.float32
    return pl.pallas_call(
        kernel,
        grid_spec=pltpu.PrefetchScalarGridSpec(
            num_scalar_prefetch=1,
            grid=(1,),
            in_specs=[pl.BlockSpec((chunk, depth), lambda j, info, at=at: (at, 0)) for _, at in flat]
            + [pl.BlockSpec(memory_space=pl.ANY)] * 2,
            out_specs=pl.BlockSpec((rows, width), lambda j, info: (0, 0)),
            scratch_shapes=[
                pltpu.VMEM((rows, width), jnp.float32),
                pltpu.VMEM((count, depth, width), jnp.bfloat16),
                pltpu.SemaphoreType.DMA((count,)),
            ],
        ),
        out_shape=jax.ShapeDtypeStruct((rows, width), kind),
        compiler_params=pltpu.CompilerParams(vmem_limit_bytes=VMEM),
        cost_estimate=work(2 * rows * depth * width * count),
        name="partial" if partial else "output",
    )(info, *[array for array, _ in flat], own_weights, weights)


def make_shards(sections, sets):
    def shards(tokens, w_query, w_key, w_value, w_out, key_start):
        rows = tokens.shape[0]
        section = lax.axis_index("sec")
        member = lax.axis_index("head")
        position = section * rows + jnp.arange(rows, dtype=jnp.int32)
        cosine, sine = tables(position)
        info = jnp.concatenate([section[None].astype(jnp.int32), key_start // SPAN])
        own = project_kv(tokens, w_key, w_value, cosine, sine)
        query = project_query(tokens, w_query, cosine, sine)
        width = w_out.shape[1] // sets
        if sets != 4 or sections != 8 or rows != 4 * SPAN:
            pieces, order = gather_sections(own, sections)
            tile = tile_rows(rows * sections)
            attended = [attend(info, query, pieces, order, at) for at in range(0, rows, tile)]
            attended = jnp.concatenate(attended, axis=0)
            terms = [
                dot(attended, w_out[:, m * width : (m + 1) * width]).astype(jnp.bfloat16)
                for m in range(sets)
            ]
            terms = jnp.concatenate(terms, axis=0)
            return lax.psum_scatter(terms, "head", scatter_dimension=0, tiled=True)

        near = [(0, 1), (3, 2)]
        middle = [(1, 2), (2, 1)]
        far = [(0, 2), (3, 1)]
        outward = [(1, 0), (2, 3)]
        left = member < 2
        half = own.shape[0] // 2
        share = w_out.shape[0] // sections
        mine = lax.dynamic_slice_in_dim(w_out, after(info, own)[0] * share, share, 0)
        quarter = [mine[:, m * width : (m + 1) * width] for m in range(4)]
        to_near = jnp.where(left, quarter[1], quarter[2])
        to_far = jnp.concatenate(
            [jnp.where(left, quarter[3], quarter[0]), jnp.where(left, quarter[2], quarter[1])], axis=1
        )
        across, down = swap(own, 2, sections), swap(own, 4, sections)
        weights = [
            lax.ppermute(to_far, "head", middle),
            lax.ppermute(to_far, "head", far),
            lax.ppermute(to_near, "head", near),
        ]
        gate = [across, down, query, *weights]
        upper, lower = after(across[:half], *gate), after(down[half:], *gate)
        beyond = [swap(upper, 4, sections), swap(lower, 2, sections)]
        mine = [after(array, upper, lower) for array in (own, across, down)]
        theirs = [swap(array, 1, sections) for array in mine]
        mine.append(after(jnp.concatenate(beyond, axis=0), *theirs))
        theirs.append(swap(mine[3], 1, sections))
        pieces, order = mine + theirs, [0, 2, 4, 6, 1, 3, 5, 7]
        for_partial = jnp.concatenate([array[:, :width] for array in weights[:2]], axis=1)
        for_partial = lax.all_gather(after(for_partial, mine[3]), "sec", axis=0, tiled=True)
        for_output = jnp.concatenate(weights[2:] + [array[:, width:] for array in weights[:2]], axis=1)
        for_output = lax.all_gather(after(for_output, theirs[3]), "sec", axis=0, tiled=True)

        chunk = tile_rows(rows * sections)
        count = rows // chunk
        held, inward, across_middle = [], [], []
        for i in range(count):
            gate = held[-1:]
            if i >= 2:
                gate = gate + [inward[i - 2], across_middle[i - 2]]
            part = attend(after(info, *gate) if gate else info, query, pieces, order, i * chunk)
            held.append(part)
            inward.append(lax.ppermute(part, "head", near))
            parcel = jnp.concatenate([part, inward[i - 1]], axis=0) if i else part
            across_middle.append(lax.ppermute(parcel, "head", middle))
        across_middle.append(lax.ppermute(inward[-1], "head", middle))

        at = jnp.stack([section, member, jnp.where(left, 0, 3)]).astype(jnp.int32)

        def sources(first, last, partial):
            sets_there = [
                [(held[i], 0) for i in range(first, last)],
                [(inward[i], 0) for i in range(first, last)],
                [(across_middle[i], 0) for i in range(first, last)],
                [(across_middle[i + 1], int(i + 1 < count)) for i in range(first, last)],
            ]
            return [sets_there[0]] + sets_there[2:] if partial else sets_there

        def partial_sum(first, last, *gate):
            found = multiply(after(at, *gate), sources(first, last, True), w_out, for_partial, 2, True)
            return found, lax.ppermute(found, "head", outward)

        def output(first, last, *gate):
            return multiply(after(at, *gate), sources(first, last, False), w_out, for_output, 1, False)

        upper, upper_sent = partial_sum(0, 2, held[3], inward[2], across_middle[2])
        third, third_sent = partial_sum(2, 3, upper)
        upper = output(0, 2, third)
        fourth, fourth_sent = partial_sum(3, 4, upper)
        lower = output(2, 4, fourth)
        partials = jnp.concatenate([upper_sent, third_sent, fourth_sent], axis=0)
        outputs = jnp.concatenate([upper, lower], axis=0)
        return (outputs + partials.astype(jnp.float32)).astype(jnp.bfloat16)

    return shards


def solution(mesh):
    placed = (
        P("sec", None),
        P(None, "head"),
        P(None, "head"),
        P(None, "head"),
        P("head", None),
        P(),
    )
    return jax.shard_map(
        make_shards(mesh.shape["sec"], mesh.shape["head"]),
        mesh=mesh,
        in_specs=placed,
        out_specs=P("sec", "head"),
        check_vma=False,
    )
```

```python
import functools
import math

import jax
import jax.numpy as jnp
from jax import lax
from jax.experimental import pallas as pl
from jax.experimental.pallas import tpu as pltpu
from jax.sharding import PartitionSpec as P

QH = 32
KVH = 8
HD = 128
SPAN = 256
GROUPS = QH // KVH
WIDE = GROUPS * HD
LOG2E = math.log2(math.e)
MIB = 1 << 20
NOTES = 32
VMEM = 60 * MIB
NEAR = 45.0


def work(flops):
    return pl.CostEstimate(flops=flops // 8, bytes_accessed=0, transcendentals=0)


def tables(position):
    midway = HD // 2
    frequency = jnp.float32(500000.0) ** (-(jnp.arange(midway, dtype=jnp.float32) * 2.0) / HD)
    angle = position.astype(jnp.float32)[:, None] * frequency[None, :]
    cosine = jnp.cos(angle)
    sine = jnp.sin(angle)
    return jnp.concatenate([cosine, cosine], axis=1), jnp.concatenate([-sine, sine], axis=1)


def turn(block, cosine, sine):
    midway = HD // 2
    swapped = jnp.concatenate([block[:, midway:], block[:, :midway]], axis=1)
    return block * cosine + swapped * sine


def dot(a, b):
    return jnp.dot(a, b, preferred_element_type=jnp.float32)


def tiles(block):
    return jnp.concatenate([block[at : at + HD].T for at in range(0, block.shape[0], HD)], axis=0)


def project_kv(tokens, w_key, w_value, cosine, sine):
    rows, depth = tokens.shape
    width = w_key.shape[1]
    tile = math.gcd(rows, 256)

    def kernel(x_ref, wk_ref, wv_ref, c_ref, s_ref, out_ref, notes):
        step = pl.program_id(0)

        @pl.when(step == 0)
        def _():
            notes[...] = jnp.zeros_like(notes)

        x = x_ref[...]
        keys = dot(x, wk_ref[...])
        values = dot(x, wv_ref[...])
        c, s = c_ref[...], s_ref[...]
        here = pl.ds(pl.multiple_of(step * tile, tile), tile)
        for h in range(0, width, HD):
            key = turn(keys[:, h : h + HD], c, s)
            value = values[:, h : h + HD]
            out_ref[here, 2 * h : 2 * h + HD] = key.astype(jnp.bfloat16)
            out_ref[here, 2 * h + HD : 2 * h + 2 * HD] = tiles(value).astype(jnp.bfloat16)
            norm = jnp.max(jnp.sqrt(jnp.sum(key * key, axis=1, keepdims=True)), axis=0, keepdims=True) * 1.02
            size = jnp.max(jnp.abs(value), axis=0, keepdims=True)
            notes[:, 2 * h : 2 * h + HD] = jnp.maximum(notes[:, 2 * h : 2 * h + HD], norm)
            notes[:, 2 * h + HD : 2 * h + 2 * HD] = jnp.maximum(
                notes[:, 2 * h + HD : 2 * h + 2 * HD], size
            )

        @pl.when(step == rows // tile - 1)
        def _():
            noted = jnp.concatenate([notes[...]] * (NOTES // 8), axis=0)
            out_ref[rows:, :] = noted.astype(jnp.bfloat16)

    return pl.pallas_call(
        kernel,
        grid=(rows // tile,),
        in_specs=[
            pl.BlockSpec((tile, depth), lambda i: (i, 0)),
            pl.BlockSpec((depth, width), lambda i: (0, 0)),
            pl.BlockSpec((depth, width), lambda i: (0, 0)),
            pl.BlockSpec((tile, HD), lambda i: (i, 0)),
            pl.BlockSpec((tile, HD), lambda i: (i, 0)),
        ],
        out_specs=pl.BlockSpec((rows + NOTES, 2 * width), lambda i: (0, 0)),
        out_shape=jax.ShapeDtypeStruct((rows + NOTES, 2 * width), jnp.bfloat16),
        scratch_shapes=[pltpu.VMEM((8, 2 * width), jnp.float32)],
        compiler_params=pltpu.CompilerParams(vmem_limit_bytes=40 * MIB),
        cost_estimate=work(4 * rows * depth * width),
        name="project_kv",
    )(tokens, w_key, w_value, cosine, sine)


def project_query(tokens, w_query, cosine, sine):
    rows, depth = tokens.shape
    width = w_query.shape[1]
    tile = math.gcd(rows, 256)

    def kernel(x_ref, w_ref, c_ref, s_ref, out_ref):
        x = x_ref[...]
        c, s = c_ref[...], s_ref[...]
        for h in range(0, width, 256):
            both = dot(x, w_ref[:, h : h + 256])
            for k in range(0, 256, HD):
                turned = tiles(turn(both[:, k : k + HD], c, s))
                out_ref[:, h + k : h + k + HD] = turned.astype(jnp.bfloat16)

    return pl.pallas_call(
        kernel,
        grid=(rows // tile,),
        in_specs=[
            pl.BlockSpec((tile, depth), lambda i: (i, 0)),
            pl.BlockSpec((depth, width), lambda i: (0, 0)),
            pl.BlockSpec((tile, HD), lambda i: (i, 0)),
            pl.BlockSpec((tile, HD), lambda i: (i, 0)),
        ],
        out_specs=pl.BlockSpec((tile, width), lambda i: (i, 0)),
        out_shape=jax.ShapeDtypeStruct((rows, width), jnp.bfloat16),
        compiler_params=pltpu.CompilerParams(vmem_limit_bytes=VMEM),
        cost_estimate=work(2 * rows * depth * width),
        name="project_query",
    )(tokens, w_query, cosine, sine)


def tile_rows(total):
    return 256 if total <= 8192 else 128


def attend(info, query, pieces, order, first):
    rows, pair_width = pieces[0].shape
    rows = rows - NOTES
    count = len(pieces)
    total = rows * count
    spans = rows // SPAN
    blocks = total // SPAN
    local_groups = pair_width // (2 * HD)
    tile = tile_rows(total)
    high = GROUPS * tile
    factor = HD**-0.5 * LOG2E

    def kernel(info_ref, q_ref, *refs):
        piece_refs = refs[:count]
        out_ref, kv, noted, scores, sums, gathered, sems, note_sems = refs[count:]
        group = pl.program_id(0)
        own = info_ref[0]
        block = own * spans + first // SPAN
        start = info_ref[1 + block]
        lowest = start // spans

        def section_copy(k, at):
            return pltpu.make_async_copy(
                piece_refs[k].at[:rows], kv.at[pl.ds(pl.multiple_of(at * rows, rows), rows)], sems.at[at]
            )

        def note_copy(k):
            return pltpu.make_async_copy(piece_refs[k].at[rows:], noted.at[k], note_sems.at[k])

        @pl.when(group == 0)
        def _():
            for k in range(count):
                note_copy(k).start()
            for k in range(count):
                at = own ^ order[k]

                @pl.when((at <= own) & (at >= lowest))
                def _():
                    section_copy(k, at).start()

            for k in range(count):
                note_copy(k).wait()

        def arrive(at):
            @pl.when(group == 0)
            def _():
                section_copy(0, at).wait()

        key_columns = pl.ds(pl.multiple_of(group * 2 * HD, HD), HD)
        value_columns = pl.ds(pl.multiple_of(group * 2 * HD + HD, HD), HD)
        q = jnp.concatenate(
            [
                q_ref[at : at + HD, h * HD : (h + 1) * HD]
                for h in range(GROUPS)
                for at in range(0, tile, HD)
            ],
            axis=1,
        )

        def score(index, size):
            keys = kv[pl.ds(pl.multiple_of(index * SPAN, SPAN), size * SPAN), key_columns]
            return dot(keys, q) * factor

        def values_at(index, size):
            return jnp.concatenate(
                [
                    kv[pl.ds(pl.multiple_of(index * SPAN + at, HD), HD), value_columns]
                    for at in range(0, size * SPAN, HD)
                ],
                axis=1,
            )

        def own_block():
            key = lax.broadcasted_iota(jnp.int32, (SPAN, high), 0)
            row = (lax.broadcasted_iota(jnp.int32, (SPAN, high), 1) & (tile - 1)) + first % SPAN
            return jnp.where(key <= row, score(block, 1), -jnp.inf)

        def fold(array, join):
            while array.shape[0] > 8:
                middle = array.shape[0] // 2
                array = join(array[:middle], array[middle:])
            return array

        def gather(weights, index, size):
            part = sums[...]
            for at in range(0, weights.shape[0], 8):
                part = part + weights[at : at + 8]
            sums[...] = part
            gathered[...] += dot(values_at(index, size), weights.astype(jnp.bfloat16))

        def others(body):
            inside = jnp.maximum(start, own * spans)

            def single(j, carry):
                body(j, 1)
                return carry

            def whole(j, carry):
                at = own - 1 - j
                arrive(at)
                body(at * spans, spans)
                return carry

            lax.fori_loop(inside, block, single, 0)
            least = (start + spans - 1) // spans
            lax.fori_loop(0, own - least, whole, 0)

            @pl.when((least > lowest) & (lowest < own))
            def _():
                arrive(lowest)
                lax.fori_loop(start, least * spans, single, 0)

        q_wide = q.astype(jnp.float32)
        q_norm = jnp.max(jnp.sum(q_wide * q_wide, axis=0, keepdims=True))
        k_norm = jnp.max(noted[:, :16, key_columns].astype(jnp.float32))
        v_size = jnp.max(noted[:, :16, value_columns].astype(jnp.float32))
        bound = q_norm * (k_norm * k_norm) * (factor * factor)
        close = (bound <= NEAR * NEAR) & (v_size <= 2.0**20) & (v_size >= 2.0**-20)
        sums[...] = jnp.zeros_like(sums)
        gathered[...] = jnp.zeros_like(gathered)
        arrive(own)

        @pl.when(close)
        def _():
            found = own_block()
            base = jnp.max(found, axis=0, keepdims=True)
            gather(jnp.exp2(found - base), block, 1)
            others(lambda index, size: gather(jnp.exp2(score(index, size) - base), index, size))

        @pl.when(jnp.logical_not(close))
        def _():
            found = own_block()
            scores[block] = found
            largest = fold(found, jnp.maximum)

            def first_pass(index, size):
                for b in range(size):
                    found = score(index + b, 1)
                    scores[index + b] = found
                    sums[...] = jnp.maximum(sums[...], fold(found, jnp.maximum))

            sums[...] = largest
            others(first_pass)
            top = jnp.max(sums[...], axis=0, keepdims=True)
            sums[...] = jnp.zeros_like(sums)

            def second_pass(j, carry):
                gather(jnp.exp2(scores[j] - top), j, 1)
                return carry

            lax.fori_loop(start, block + 1, second_pass, 0)

        result = gathered[...] / jnp.sum(sums[...], axis=0, keepdims=True)
        for h in range(GROUPS):
            for at in range(0, tile, HD):
                part = result[:, h * tile + at : h * tile + at + HD]
                out_ref[at : at + HD, h * HD : (h + 1) * HD] = part.T.astype(jnp.bfloat16)

    return pl.pallas_call(
        kernel,
        grid_spec=pltpu.PrefetchScalarGridSpec(
            num_scalar_prefetch=1,
            grid=(local_groups,),
            in_specs=[pl.BlockSpec((tile, WIDE), lambda g, info: (first // tile, g))]
            + [pl.BlockSpec(memory_space=pl.ANY)] * count,
            out_specs=pl.BlockSpec((tile, WIDE), lambda g, info: (0, g)),
            scratch_shapes=[
                pltpu.VMEM((total, pair_width), jnp.bfloat16),
                pltpu.VMEM((count, NOTES, pair_width), jnp.bfloat16),
                pltpu.VMEM((blocks, SPAN, high), jnp.float32),
                pltpu.VMEM((8, high), jnp.float32),
                pltpu.VMEM((HD, high), jnp.float32),
                pltpu.SemaphoreType.DMA((count,)),
                pltpu.SemaphoreType.DMA((count,)),
            ],
        ),
        out_shape=jax.ShapeDtypeStruct((tile, local_groups * WIDE), jnp.bfloat16),
        compiler_params=pltpu.CompilerParams(vmem_limit_bytes=VMEM),
        cost_estimate=work(tile * local_groups * GROUPS * total * HD * 4),
        name="attend",
    )(info, query, *pieces)


def swap(array, bit, size):
    return lax.ppermute(array, "sec", [(i, i ^ bit) for i in range(size)])


def gather_sections(own, size, second=None, third=None):
    if size == 8:
        half = own.shape[0] // 2
        across = swap(own, 2, size)
        down = swap(own, 4, size)
        upper, lower = across[:half], down[half:]
        if second:
            waited = second(across, down)
            if waited:
                upper, lower = after(upper, *waited), after(lower, *waited)
        far = jnp.concatenate([swap(upper, 4, size), swap(lower, 2, size)], axis=0)
        mine = [own, across, down, far]
        if third:
            waited = third(far)
            mine = [after(a, *waited) for a in mine]
        return mine + [swap(a, 1, size) for a in mine], [0, 2, 4, 6, 1, 3, 5, 7]
    held, order = [own], [0]
    bit = 1
    while bit < size:
        held = held + [swap(a, bit, size) for a in held]
        order = order + [k ^ bit for k in order]
        bit *= 2
    return held, order


def after(array, *others):
    def kernel(*refs):
        pass

    return pl.pallas_call(
        kernel,
        in_specs=[pl.BlockSpec(memory_space=pl.ANY)] * (1 + len(others)),
        out_specs=pl.BlockSpec(memory_space=pl.ANY),
        out_shape=jax.ShapeDtypeStruct(array.shape, array.dtype),
        input_output_aliases={0: 0},
        name="after",
    )(array, *others)


def multiply(info, sources, own_weights, weights, own_column, partial):
    chunks = len(sources[0])
    depth, width = own_weights.shape[0], own_weights.shape[1] // 4
    chunk = sources[0][0][0].shape[0]
    count = len(sources)
    flat = [entry for source in sources for entry in source]

    def kernel(info_ref, *refs):
        source_refs = refs[: len(flat)]
        own_ref, weight_ref, out_ref, total, held, sems = refs[len(flat) :]
        own_at = pl.multiple_of(info_ref[own_column] * width, width)
        copies = [pltpu.make_async_copy(own_ref.at[:, pl.ds(own_at, width)], held.at[0], sems.at[0])]
        for n in range(1, count):
            block = weight_ref.at[:, (n - 1) * width : n * width]
            copies.append(pltpu.make_async_copy(block, held.at[n], sems.at[n]))
        for copy in copies:
            copy.start()
        for n, copy in enumerate(copies):
            copy.wait()
            for c in range(chunks):
                part = slice(c * chunk, (c + 1) * chunk)
                term = dot(source_refs[n * chunks + c][...], held[n])
                term = term.astype(jnp.bfloat16).astype(jnp.float32)
                if n == 0:
                    total[part] = term
                elif n < count - 1:
                    total[part] += term
                else:
                    out_ref[part] = (total[part] + term).astype(out_ref.dtype)

    rows = chunk * chunks
    kind = jnp.bfloat16 if partial else jnp.float32
    return pl.pallas_call(
        kernel,
        grid_spec=pltpu.PrefetchScalarGridSpec(
            num_scalar_prefetch=1,
            grid=(1,),
            in_specs=[pl.BlockSpec((chunk, depth), lambda j, info, at=at: (at, 0)) for _, at in flat]
            + [pl.BlockSpec(memory_space=pl.ANY)] * 2,
            out_specs=pl.BlockSpec((rows, width), lambda j, info: (0, 0)),
            scratch_shapes=[
                pltpu.VMEM((rows, width), jnp.float32),
                pltpu.VMEM((count, depth, width), jnp.bfloat16),
                pltpu.SemaphoreType.DMA((count,)),
            ],
        ),
        out_shape=jax.ShapeDtypeStruct((rows, width), kind),
        compiler_params=pltpu.CompilerParams(vmem_limit_bytes=VMEM),
        cost_estimate=work(2 * rows * depth * width * count),
        name="partial" if partial else "output",
    )(info, *[array for array, _ in flat], own_weights, weights)


def make_shards(sections, sets):
    def shards(tokens, w_query, w_key, w_value, w_out, key_start):
        rows = tokens.shape[0]
        section = lax.axis_index("sec")
        member = lax.axis_index("head")
        position = section * rows + jnp.arange(rows, dtype=jnp.int32)
        cosine, sine = tables(position)
        info = jnp.concatenate([section[None].astype(jnp.int32), key_start // SPAN])
        own = project_kv(tokens, w_key, w_value, cosine, sine)
        query = project_query(tokens, w_query, cosine, sine)
        width = w_out.shape[1] // sets
        if sets != 4 or sections != 8 or rows != 4 * SPAN:
            pieces, order = gather_sections(own, sections)
            tile = tile_rows(rows * sections)
            attended = [attend(info, query, pieces, order, at) for at in range(0, rows, tile)]
            attended = jnp.concatenate(attended, axis=0)
            terms = [
                dot(attended, w_out[:, m * width : (m + 1) * width]).astype(jnp.bfloat16)
                for m in range(sets)
            ]
            terms = jnp.concatenate(terms, axis=0)
            return lax.psum_scatter(terms, "head", scatter_dimension=0, tiled=True)

        near = [(0, 1), (3, 2)]
        middle = [(1, 2), (2, 1)]
        far = [(0, 2), (3, 1)]
        outward = [(1, 0), (2, 3)]
        left = member < 2
        half = own.shape[0] // 2
        share = w_out.shape[0] // sections
        mine = lax.dynamic_slice_in_dim(w_out, after(info, own)[0] * share, share, 0)
        quarter = [mine[:, m * width : (m + 1) * width] for m in range(4)]
        to_near = jnp.where(left, quarter[1], quarter[2])
        to_far = jnp.concatenate(
            [jnp.where(left, quarter[3], quarter[0]), jnp.where(left, quarter[2], quarter[1])], axis=1
        )
        across, down = swap(own, 2, sections), swap(own, 4, sections)
        weights = [
            lax.ppermute(to_far, "head", middle),
            lax.ppermute(to_far, "head", far),
            lax.ppermute(to_near, "head", near),
        ]
        gate = [across, down, query, *weights]
        upper, lower = after(across[:half], *gate), after(down[half:], *gate)
        beyond = [swap(upper, 4, sections), swap(lower, 2, sections)]
        mine = [after(array, upper, lower) for array in (own, across, down)]
        theirs = [swap(array, 1, sections) for array in mine]
        mine.append(after(jnp.concatenate(beyond, axis=0), *theirs))
        theirs.append(swap(mine[3], 1, sections))
        pieces, order = mine + theirs, [0, 2, 4, 6, 1, 3, 5, 7]
        for_partial = jnp.concatenate([array[:, :width] for array in weights[:2]], axis=1)
        for_partial = lax.all_gather(after(for_partial, mine[3]), "sec", axis=0, tiled=True)
        for_output = jnp.concatenate(weights[2:] + [array[:, width:] for array in weights[:2]], axis=1)
        for_output = lax.all_gather(after(for_output, theirs[3]), "sec", axis=0, tiled=True)

        chunk = tile_rows(rows * sections)
        count = rows // chunk
        held, inward, across_middle = [], [], []
        for i in range(count):
            gate = held[-1:]
            if i >= 2:
                gate = gate + [inward[i - 2], across_middle[i - 2]]
            part = attend(after(info, *gate) if gate else info, query, pieces, order, i * chunk)
            held.append(part)
            inward.append(lax.ppermute(part, "head", near))
            parcel = jnp.concatenate([part, inward[i - 1]], axis=0) if i else part
            across_middle.append(lax.ppermute(parcel, "head", middle))

        at = jnp.stack([section, member, jnp.where(left, 0, 3)]).astype(jnp.int32)

        def sources(first, last, partial):
            sets_there = [
                [(held[i], 0) for i in range(first, last)],
                [(inward[i], 0) for i in range(first, last)],
                [(across_middle[i], 0) for i in range(first, last)],
                [(across_middle[i + 1], int(i + 1 < count)) for i in range(first, last)],
            ]
            return [sets_there[0]] + sets_there[2:] if partial else sets_there

        def partial_sum(first, last, *gate):
            found = multiply(after(at, *gate), sources(first, last, True), w_out, for_partial, 2, True)
            return found, lax.ppermute(found, "head", outward)

        def output(first, last, *gate):
            return multiply(after(at, *gate), sources(first, last, False), w_out, for_output, 1, False)

        upper, upper_sent = partial_sum(0, 2, held[3], inward[2], across_middle[2])
        inward[3] = after(inward[3], upper)
        across_middle.append(lax.ppermute(inward[3], "head", middle))
        upper = output(0, 2, upper)
        third, third_sent = partial_sum(2, 3, upper)
        fourth, fourth_sent = partial_sum(3, 4, third)
        lower = output(2, 4, fourth)
        partials = jnp.concatenate([upper_sent, third_sent, fourth_sent], axis=0)
        outputs = jnp.concatenate([upper, lower], axis=0)
        return (outputs + partials.astype(jnp.float32)).astype(jnp.bfloat16)

    return shards


def solution(mesh):
    placed = (
        P("sec", None),
        P(None, "head"),
        P(None, "head"),
        P(None, "head"),
        P("head", None),
        P(),
    )
    return jax.shard_map(
        make_shards(mesh.shape["sec"], mesh.shape["head"]),
        mesh=mesh,
        in_specs=placed,
        out_specs=P("sec", "head"),
        check_vma=False,
    )
```
